256 devices in a mesh: blk: 64 (over x, z, y_lo), narrow: 4 (over y_hi, core).
Axes of the slice: x: 4, y: 4 (y_hi: 2, y_lo: 2; y = y_hi * 2 + y_lo), z: 8, core: 2. Of those that a mesh axis runs over, the one named last changes fastest.
Arguments:
- embed_low: bfloat16 [32768, 384], P(('blk', 'narrow')), may hold values from -0.3125 to 0.3125
- embed_high: bfloat16 [32768, 384], P(('blk', 'narrow')), may hold values from -0.3125 to 0.3125
- partner: int32 [32768], P(('blk', 'narrow')), may hold values from 0 to 32767, each once
- log_scale: float32 [], replicated, may hold values from 3 to 4.1
- bias: float32 [], replicated, may hold values from -6 to -4
Outputs:
- grad_low: float32 [32768, 384], P(('blk', 'narrow'))
- grad_high: float32 [32768, 384], P(('blk', 'narrow'))
The draws below stay inside these ranges and needn't reach their ends.
Inputs may be any that keep to these rules, and one draw needn't show every extreme that they name: Each 40x crop is the partner of exactly one 10x crop.
All inputs are finite; a program needn't handle non-finite values.
Results may differ from the reference program's by a relative error of at most 0.00065.
Values may be sent and summed in bfloat16 or wider, within the bound.
A program may use at most 64 MiB of HBM per device.

```python
import math
import jax
import jax.numpy as jnp
from jax import lax

D = 384
N = 32768


def levels(stream_key, dims, shards, low, high):
    level, own = 1.0, jax.random.fold_in(stream_key, 6)
    for dim, blocks in shards:
        heights = jnp.exp(jax.random.uniform(jax.random.fold_in(own, dim), (blocks,), jnp.float32, low / len(shards), high / len(shards)))
        level = level * jnp.repeat(heights, dims[dim] // blocks).reshape([-1 if axis == dim else 1 for axis in range(len(dims))])
    return level


def bell_draw(key, dims, scale, limit, split=(), dtype=jnp.bfloat16):
    loudness = levels(key, dims, split, -0.22, 0.18) if split else 1.0
    values = jax.random.normal(key, dims, jnp.float32) * scale * loudness
    return jnp.minimum(jnp.maximum(values, -limit), limit).astype(dtype)


def setup_inputs(seed: int = 0) -> dict:
    streams_of = jax.random.split(jax.random.key(seed), 6)
    embed_low = bell_draw(streams_of[0], (N, D), (D ** -0.5), 0.3125, ((0, 256),))
    embed_high = bell_draw(streams_of[1], (N, D), (D ** -0.5), 0.3125, ((0, 256),))
    partner = jax.random.permutation(streams_of[2], N).astype(jnp.int32)
    log_scale = jnp.clip(jax.random.uniform(streams_of[3], (), jnp.float32, 3.0, 4.1), 3.0, 4.1)
    bias = jnp.clip(jax.random.uniform(streams_of[4], (), jnp.float32, -6.0, -4.0), -6.0, -4.0)
    return {"embed_low": embed_low, "embed_high": embed_high, "partner": partner, "log_scale": log_scale, "bias": bias}


def reference(embed_low, embed_high, partner, log_scale, bias):
    scale = jnp.exp(log_scale.astype(jnp.float32))
    count = embed_low.shape[0]
    width = embed_low.shape[1]
    height = math.gcd(count, 512)
    low_blocks = embed_low.reshape(count // height, height, width)
    partner_blocks = partner.reshape(count // height, height)
    columns = lax.iota(jnp.int32, count)

    def visit(total, item):
        rows, targets = item
        logits = scale * lax.dot_general(rows, embed_high, (((1,), (1,)), ((), ())), preferred_element_type=jnp.float32) + bias
        match = (targets[:, None] == columns[None, :]).astype(jnp.float32)
        weights = (scale * (jax.nn.sigmoid(logits) - match)).astype(jnp.bfloat16)
        low_term = jnp.dot(weights, embed_high, preferred_element_type=jnp.float32)
        high_term = lax.dot_general(weights, rows, (((0,), (0,)), ((), ())), preferred_element_type=jnp.float32)
        return total + high_term, low_term

    total, grad_low = lax.scan(visit, jnp.zeros((count, width), jnp.float32), (low_blocks, partner_blocks))
    return grad_low.reshape(count, width), total
```

```python
import functools

import jax
import jax.numpy as jnp
from jax import lax
from jax.experimental import pallas as pl
from jax.experimental.pallas import tpu as pltpu
from jax.sharding import PartitionSpec as P

MESH = pl.DeviceIdType.MESH
F32, BF16 = jnp.float32, jnp.bfloat16
X, Y, Z = 4, 4, 8
ROWS, WIDTH = 128, 384
HALF = WIDTH // 2

NEAR = [(0, 0), (1, 0), (3, 0), (0, 1), (0, 3), (2, 0), (0, 2)]
FAR = [(1, 1), (3, 3), (1, 3), (3, 1), (2, 1), (1, 2), (2, 3), (3, 2), (2, 2)]
LOW_AT = {slot: i for i, slot in enumerate(NEAR + FAR)}
HIGH_AT = {(dz, dc): 2 * i + dc for i, dz in enumerate((0, 1, 7, 2, 6, 3, 5, 4)) for dc in (0, 1)}
GROUP = 8
BLOCK = GROUP * ROWS


def dot(a, b, over):
    return lax.dot_general(a, b, (over, ((), ())), preferred_element_type=F32)


def kernel(
    low_in, high_in, partner_in, factors,
    low_out, high_out,
    low, high, part, prow, weights, gl, gh,
    got_a, got_b, sum_a, sum_b, last_a, last_b,
    got_core, got_three, got_four, got_two, got_one,
    send_sems, recv_sems,
):
    blk, narrow = lax.axis_index("blk"), lax.axis_index("narrow")
    x, z, y, core = blk // 16, (blk // 2) % 8, (narrow // 2) * 2 + blk % 2, narrow % 2

    def device(dx=0, dy=0, dz=0, dc=0):
        px, py, pz, pc = (x + dx) % X, (y + dy) % Y, (z + dz) % Z, (core + dc) % 2
        return ((px * Z + pz) * 2 + py % 2, (py // 2) * 2 + pc)

    copies = []

    def send(src, dst, **to):
        k = len(copies)
        copy = pltpu.make_async_remote_copy(
            src, dst, send_sems.at[k], recv_sems.at[k], device_id=device(**to), device_id_type=MESH
        )
        copy.start()
        copies.append(copy)
        return copy

    def low_rows(slot, first=0, count=ROWS):
        return pl.ds(LOW_AT[slot] * ROWS + first, count)

    def low_cols(slot):
        return pl.ds(LOW_AT[slot] * ROWS, ROWS)

    def high_rows(dz, dc, first=0, count=ROWS):
        return pl.ds(HIGH_AT[dz, dc] * ROWS + first, count)

    a_rows, b_rows = pl.ds(0, HALF), pl.ds(HALF, HALF)

    peers = [dict(dx=e) for e in (1, 2, 3)] + [dict(dy=e) for e in (1, 2, 3)]
    peers += [dict(dz=e) for e in (1, 2, 6, 7)] + [dict(dc=1)]
    barrier = pltpu.get_barrier_semaphore()
    for peer in peers:
        pl.semaphore_signal(barrier, inc=1, device_id=device(**peer), device_id_type=MESH)
    low[low_rows((0, 0)), :] = low_in[...]
    high[high_rows(0, 0), :] = high_in[...]
    part[0, 0] = jnp.broadcast_to(partner_in[...], (8, ROWS))
    pl.semaphore_wait(barrier, len(peers))

    low_x, low_y, low_a, low_b, part_x, part_y, high_same, high_other = {}, {}, {}, {}, {}, {}, {}, {}
    for e in (2, 6):
        high_same[8 - e] = send(high_in, high.at[high_rows(8 - e, 0)], dz=e)
    for e in (1, 3):
        part_x[4 - e] = send(part.at[0, 0], part.at[0, 4 - e], dx=e)
        low_x[4 - e] = send(low_in, low.at[low_rows((4 - e, 0))], dx=e)
        low_y[4 - e] = send(low_in, low.at[low_rows((0, 4 - e))], dy=e)
    high_other[0] = send(high_in, high.at[high_rows(0, 1)], dc=1)
    for e in (1, 7):
        high_same[8 - e] = send(high_in, high.at[high_rows(8 - e, 0)], dz=e)
    part_x[2] = send(part.at[0, 0], part.at[0, 2], dx=2)
    low_x[2] = send(low_in, low.at[low_rows((2, 0))], dx=2)
    low_y[2] = send(low_in, low.at[low_rows((0, 2))], dy=2)

    def to_other_core(dz):
        rows = high_rows(dz, 0)
        high_other[dz] = send(high.at[rows], high.at[high_rows(dz, 1)], dc=1)

    def pass_low(d):
        low_x[d].wait_recv()
        for e in (1, 3, 2):
            src = low.at[low_rows((d, 0), 0, 64)]
            low_a[d, 4 - e] = send(src, low.at[low_rows((d, 4 - e), 0, 64)], dy=e)
        low_y[d].wait_recv()
        for e in (1, 3, 2):
            src = low.at[low_rows((0, d), 64, 64)]
            low_b[4 - e, d] = send(src, low.at[low_rows((4 - e, d), 64, 64)], dx=e)

    pass_low(1)
    pass_low(3)
    for e in (1, 3, 2):
        part_x[e].wait_recv()
    for e in (1, 3, 2):
        part_y[4 - e] = send(part.at[0], part.at[4 - e], dy=e)
    high_same[6].wait_recv()
    high_same[5] = send(high.at[high_rows(6, 0)], high.at[high_rows(5, 0)], dz=1)
    four_a = send(high.at[high_rows(6, 0, 0, 64)], high.at[high_rows(4, 0, 0, 64)], dz=2)
    high_same[2].wait_recv()
    high_same[3] = send(high.at[high_rows(2, 0)], high.at[high_rows(3, 0)], dz=7)
    four_b = send(high.at[high_rows(2, 0, 64, 64)], high.at[high_rows(4, 0, 64, 64)], dz=6)
    pass_low(2)
    to_other_core(2)
    to_other_core(6)
    for dz in (1, 7):
        high_same[dz].wait_recv()
        to_other_core(dz)

    scale, bias = factors[0], factors[1]
    gain, shift, half = 0.5 * scale, 0.5 * bias, 0.5 * scale
    started = set()

    def add_to(ref, index, key, value):
        if key in started:
            ref[index] += value
        else:
            ref[index] = value
            started.add(key)

    def block(lg, hg):
        cols, rows = pl.ds(lg * BLOCK, BLOCK), pl.ds(hg * BLOCK, BLOCK)
        low_block, high_block = low[cols, :], high[rows, :]
        logits = dot(high_block, low_block, ((1,), (1,)))
        wanted = prow[:, cols]
        for i in range(GROUP):
            dz, dc = next(k for k, v in HIGH_AT.items() if v == hg * GROUP + i)
            b, n = device(dz=dz, dc=dc)
            first = (b * 4 + n) * ROWS
            here = slice(i * ROWS, (i + 1) * ROWS)
            ids = lax.broadcasted_iota(jnp.int32, (ROWS, BLOCK), 0)
            match = ids == wanted - first
            value = jnp.tanh(logits[here] * gain + shift) * half + jnp.where(match, -half, half)
            weights[here, :] = value.astype(BF16)
        w = weights[...]
        add_to(gh, (rows, slice(None)), ("h", hg), dot(w, low_block, ((1,), (0,))))
        add_to(gl, (slice(None), cols), ("l", lg), dot(high_block, w, ((0,), (0,))))

    def take_part(slots):
        for dx, dy in slots:
            prow[:, low_cols((dx, dy))] = part[dy, dx, 0:1, :]

    high_other[0].wait_recv()
    for dz in (1, 7, 2):
        high_other[dz].wait_recv()
    low_a[1, 1].wait_recv()
    low_b[1, 1].wait_recv()
    for e in (1, 2, 3):
        part_y[e].wait_recv()
    take_part(NEAR + FAR)
    block(0, 0)
    for dz in (3, 5):
        high_same[dz].wait_recv()
        to_other_core(dz)
    four_a.wait_recv()
    four_b.wait_recv()
    to_other_core(4)
    for slot in FAR[1:]:
        low_a[slot].wait_recv()
        low_b[slot].wait_recv()
    for dz in (6, 3, 5, 4):
        high_other[dz].wait_recv()
    block(1, 1)
    block(0, 1)

    from_core = {}

    def core_sum_send(dz):
        from_core[dz] = send(gh.at[high_rows(dz, 1)], got_core.at[dz], dc=1)

    def core_sum_take(dz):
        from_core[dz].wait_recv()
        gh[high_rows(dz, 0), :] += got_core[dz]

    for dz in (4, 3, 5, 6):
        core_sum_send(dz)
    block(1, 0)
    for dz in (2, 1, 7, 0):
        core_sum_send(dz)

    a_far, b_far, a_near, b_near = {}, {}, {}, {}
    for e in (1, 3, 2):
        for d in (2, 1, 3, 0):
            a_far[4 - e, d] = send(gl.at[a_rows, low_cols((d, e))], got_a.at[4 - e, d], dy=e)
            b_far[4 - e, d] = send(gl.at[b_rows, low_cols((e, d))], got_b.at[4 - e, d], dx=e)

    for dz in (4, 3, 5, 6, 2):
        core_sum_take(dz)
    four_a = send(gh.at[high_rows(4, 0, 0, 64)], got_four.at[0], dz=2)
    four_b = send(gh.at[high_rows(4, 0, 64, 64)], got_four.at[1], dz=6)
    three_a = send(gh.at[high_rows(3, 0)], got_three.at[0], dz=1)
    three_b = send(gh.at[high_rows(5, 0)], got_three.at[1], dz=7)
    for dz in (1, 7):
        core_sum_take(dz)
    one_a = send(gh.at[high_rows(1, 0)], got_one.at[0], dz=1)
    one_b = send(gh.at[high_rows(7, 0)], got_one.at[1], dz=7)

    three_a.wait_recv()
    four_a.wait_recv()
    gh[high_rows(2, 0), :] += got_three[0]
    gh[high_rows(2, 0, 0, 64), :] += got_four[0]
    two_a = send(gh.at[high_rows(2, 0)], got_two.at[0], dz=2)
    three_b.wait_recv()
    four_b.wait_recv()
    gh[high_rows(6, 0), :] += got_three[1]
    gh[high_rows(6, 0, 64, 64), :] += got_four[1]
    two_b = send(gh.at[high_rows(6, 0)], got_two.at[1], dz=6)

    for d in (2, 1, 3):
        for e in (1, 3, 2):
            a_far[e, d].wait_recv()
            b_far[e, d].wait_recv()
        sum_a[d] = gl[a_rows, low_cols((d, 0))] + got_a[1, d] + got_a[2, d] + got_a[3, d]
        a_near[d] = send(sum_a.at[d], last_a.at[d], dx=d)
        sum_b[d] = gl[b_rows, low_cols((0, d))] + got_b[1, d] + got_b[2, d] + got_b[3, d]
        b_near[d] = send(sum_b.at[d], last_b.at[d], dy=d)

    core_sum_take(0)
    for copy in (one_a, one_b, two_a, two_b):
        copy.wait_recv()
    high_out[...] = gh[high_rows(0, 0), :] + got_one[0] + got_one[1] + got_two[0] + got_two[1]
    for e in (1, 3, 2):
        a_far[e, 0].wait_recv()
        b_far[e, 0].wait_recv()
    for d in (1, 3, 2):
        a_near[d].wait_recv()
        b_near[d].wait_recv()
    total_a = gl[a_rows, low_cols((0, 0))] + got_a[1, 0] + got_a[2, 0] + got_a[3, 0]
    total_a += last_a[1] + last_a[2] + last_a[3]
    total_b = gl[b_rows, low_cols((0, 0))] + got_b[1, 0] + got_b[2, 0] + got_b[3, 0]
    total_b += last_b[1] + last_b[2] + last_b[3]
    low_out[...] = jnp.concatenate([total_a, total_b], axis=0).T
    for copy in copies:
        copy.wait_send()


def per_device(embed_low, embed_high, partner, log_scale, bias):
    factors = jnp.stack([jnp.exp(log_scale), bias])
    vmem, smem = pl.BlockSpec(memory_space=pltpu.VMEM), pl.BlockSpec(memory_space=pltpu.SMEM)
    group = 2 * BLOCK
    grad = jax.ShapeDtypeStruct((ROWS, WIDTH), F32)
    return pl.pallas_call(
        kernel,
        out_shape=(grad, grad),
        in_specs=[vmem, vmem, vmem, smem],
        out_specs=(vmem, vmem),
        scratch_shapes=[
            pltpu.VMEM((group, WIDTH), BF16),
            pltpu.VMEM((group, WIDTH), BF16),
            pltpu.VMEM((4, 4, 8, ROWS), jnp.int32),
            pltpu.VMEM((1, group), jnp.int32),
            pltpu.VMEM((BLOCK, BLOCK), BF16),
            pltpu.VMEM((WIDTH, group), F32),
            pltpu.VMEM((group, WIDTH), F32),
            pltpu.VMEM((4, 4, HALF, ROWS), F32),
            pltpu.VMEM((4, 4, HALF, ROWS), F32),
            pltpu.VMEM((4, HALF, ROWS), F32),
            pltpu.VMEM((4, HALF, ROWS), F32),
            pltpu.VMEM((4, HALF, ROWS), F32),
            pltpu.VMEM((4, HALF, ROWS), F32),
            pltpu.VMEM((8, ROWS, WIDTH), F32),
            pltpu.VMEM((2, ROWS, WIDTH), F32),
            pltpu.VMEM((2, ROWS // 2, WIDTH), F32),
            pltpu.VMEM((2, ROWS, WIDTH), F32),
            pltpu.VMEM((2, ROWS, WIDTH), F32),
            pltpu.SemaphoreType.DMA((96,)),
            pltpu.SemaphoreType.DMA((96,)),
        ],
        compiler_params=pltpu.CompilerParams(
            collective_id=0, has_side_effects=True, vmem_limit_bytes=56 * 2**20
        ),
    )(embed_low, embed_high, partner.reshape(1, ROWS), factors)


def solution(mesh):
    in_specs = (
        P(("blk", "narrow"), None),
        P(("blk", "narrow"), None),
        P(("blk", "narrow")),
        P(),
        P(),
    )
    out_specs = (P(("blk", "narrow"), None), P(("blk", "narrow"), None))
    return jax.shard_map(
        per_device, mesh=mesh, in_specs=in_specs, out_specs=out_specs, check_vma=False
    )
```

```python
import functools

import jax
import jax.numpy as jnp
from jax import lax
from jax.experimental import pallas as pl
from jax.experimental.pallas import tpu as pltpu
from jax.sharding import PartitionSpec as P

MESH = pl.DeviceIdType.MESH
F32, BF16 = jnp.float32, jnp.bfloat16
X, Y, Z = 4, 4, 8
ROWS, WIDTH = 128, 384
HALF = WIDTH // 2

NEAR = [(0, 0), (1, 0), (3, 0), (0, 1), (0, 3), (2, 0), (0, 2), (1, 1)]
FAR = [(3, 3), (1, 3), (3, 1), (2, 1), (1, 2), (2, 3), (3, 2), (2, 2)]
LOW_AT = {slot: i for i, slot in enumerate(NEAR + FAR)}
HIGH_AT = {(dz, dc): 2 * i + dc for i, dz in enumerate((0, 1, 7, 2, 6, 3, 5, 4)) for dc in (0, 1)}
TAIL = 16
STEPS = 32767.0


def dot(a, b, over):
    return lax.dot_general(a, b, (over, ((), ())), preferred_element_type=F32)


def encode(ref, value):
    rows = value.shape[0]
    top = jnp.maximum(jnp.max(jnp.abs(value), axis=0, keepdims=True), 1e-30)
    exponent = jnp.ceil(jnp.log2(top))
    ref[0:rows, :] = jnp.round(value * (STEPS * jnp.exp2(-exponent))).astype(jnp.int32).astype(jnp.int16)
    ref[rows : rows + TAIL, :] = jnp.broadcast_to(exponent, (TAIL, value.shape[1])).astype(jnp.int32).astype(jnp.int16)


def decode(ref):
    rows = ref.shape[0] - TAIL
    exponent = ref[rows : rows + TAIL, :].astype(jnp.int32).astype(F32)[0:1]
    return ref[0:rows, :].astype(jnp.int32).astype(F32) * (jnp.exp2(exponent) * (1.0 / STEPS))


def kernel(
    low_in, high_in, partner_in, log_scale, bias_in,
    low_out, high_out,
    low, high, part, prow, weights, gl, gh,
    ship_a, ship_b, got_a, got_b, next_a, next_b, last_a, last_b,
    got_core, ship_three, ship_four, ship_two, ship_one, got_three, got_four, got_two, got_one,
    load_sems, send_sems, recv_sems,
):
    blk, narrow = lax.axis_index("blk"), lax.axis_index("narrow")
    x, z, y, core = blk // 16, (blk // 2) % 8, (narrow // 2) * 2 + blk % 2, narrow % 2

    def device(dx=0, dy=0, dz=0, dc=0):
        px, py, pz, pc = (x + dx) % X, (y + dy) % Y, (z + dz) % Z, (core + dc) % 2
        return ((px * Z + pz) * 2 + py % 2, (py // 2) * 2 + pc)

    copies = []

    def send(src, dst, **to):
        k = len(copies)
        copy = pltpu.make_async_remote_copy(
            src, dst, send_sems.at[k], recv_sems.at[k], device_id=device(**to), device_id_type=MESH
        )
        copy.start()
        copies.append(copy)
        return copy

    def low_rows(slot, first=0, count=ROWS):
        return pl.ds(LOW_AT[slot] * ROWS + first, count)

    def low_cols(slot):
        return pl.ds(LOW_AT[slot] * ROWS, ROWS)

    def high_rows(dz, dc, first=0, count=ROWS):
        return pl.ds(HIGH_AT[dz, dc] * ROWS + first, count)

    a_rows, b_rows = pl.ds(0, HALF), pl.ds(HALF, HALF)
    own_low, own_high = low.at[low_rows((0, 0))], high.at[high_rows(0, 0)]
    loads = [(low_in, own_low), (high_in, own_high), (partner_in, part.at[0, 0])]
    loads = [pltpu.make_async_copy(src, dst, load_sems.at[i]) for i, (src, dst) in enumerate(loads)]
    for load in loads:
        load.start()

    peers = [dict(dx=e) for e in (1, 2, 3)] + [dict(dy=e) for e in (1, 2, 3)]
    peers += [dict(dz=e) for e in (1, 2, 6, 7)] + [dict(dc=1)]
    barrier = pltpu.get_barrier_semaphore()
    for peer in peers:
        pl.semaphore_signal(barrier, inc=1, device_id=device(**peer), device_id_type=MESH)
    for load in loads:
        load.wait()
    scale = jnp.exp(jnp.full((1, 512), log_scale[0, 0], F32))
    gain, shift, half = 0.5 * scale, 0.5 * bias_in[0, 0], 0.5 * scale
    pl.semaphore_wait(barrier, len(peers))

    low_x, low_y, low_a, low_b, part_x, part_y, high_same, high_other = {}, {}, {}, {}, {}, {}, {}, {}
    for e in (1, 3):
        low_x[4 - e] = send(own_low, low.at[low_rows((4 - e, 0))], dx=e)
        low_y[4 - e] = send(own_low, low.at[low_rows((0, 4 - e))], dy=e)
    for e in (2, 6):
        high_same[8 - e] = send(own_high, high.at[high_rows(8 - e, 0)], dz=e)
    low_x[2] = send(own_low, low.at[low_rows((2, 0))], dx=2)
    low_y[2] = send(own_low, low.at[low_rows((0, 2))], dy=2)
    for e in (1, 7):
        high_same[8 - e] = send(own_high, high.at[high_rows(8 - e, 0)], dz=e)
    high_other[0] = send(own_high, high.at[high_rows(0, 1)], dc=1)
    for e in (1, 3, 2):
        part_x[4 - e] = send(part.at[0, 0], part.at[0, 4 - e], dx=e)

    def to_other_core(dz):
        rows = high_rows(dz, 0)
        high_other[dz] = send(high.at[rows], high.at[high_rows(dz, 1)], dc=1)

    def pass_low(d):
        low_x[d].wait_recv()
        for e in (1, 3, 2):
            src = low.at[low_rows((d, 0), 0, 64)]
            low_a[d, 4 - e] = send(src, low.at[low_rows((d, 4 - e), 0, 64)], dy=e)
        low_y[d].wait_recv()
        for e in (1, 3, 2):
            src = low.at[low_rows((0, d), 64, 64)]
            low_b[4 - e, d] = send(src, low.at[low_rows((4 - e, d), 64, 64)], dx=e)

    pass_low(1)
    pass_low(3)
    pass_low(2)
    high_same[6].wait_recv()
    high_same[5] = send(high.at[high_rows(6, 0)], high.at[high_rows(5, 0)], dz=1)
    four_a = send(high.at[high_rows(6, 0, 0, 64)], high.at[high_rows(4, 0, 0, 64)], dz=2)
    high_same[2].wait_recv()
    high_same[3] = send(high.at[high_rows(2, 0)], high.at[high_rows(3, 0)], dz=7)
    four_b = send(high.at[high_rows(2, 0, 64, 64)], high.at[high_rows(4, 0, 64, 64)], dz=6)
    for e in (1, 3, 2):
        part_x[e].wait_recv()
    for e in (1, 3, 2):
        part_y[4 - e] = send(part.at[0], part.at[4 - e], dy=e)
    for dz in (1, 7):
        high_same[dz].wait_recv()
        to_other_core(dz)
    to_other_core(2)
    to_other_core(6)

    started = set()

    def add_to(ref, index, keys, value):
        if keys <= started:
            ref[index] += value
        else:
            ref[index] = value
            started.update(keys)

    def block(low_slots, high_slots):
        first_low, first_high = LOW_AT[low_slots[0]], HIGH_AT[high_slots[0]]
        wide, tall = len(low_slots) * ROWS, len(high_slots) * ROWS
        cols, rows = pl.ds(first_low * ROWS, wide), pl.ds(first_high * ROWS, tall)
        low_block, high_block = low[cols, :], high[rows, :]
        logits = dot(high_block, low_block, ((1,), (1,)))
        wanted = prow[:, cols]
        for i, (dz, dc) in enumerate(high_slots):
            b, n = device(dz=dz, dc=dc)
            local = wanted - (b * 4 + n) * ROWS
            ids = lax.broadcasted_iota(jnp.int32, (ROWS, 512), 0)
            for left in range(0, wide, 512):
                here = (slice(i * ROWS, (i + 1) * ROWS), slice(left, left + 512))
                match = ids == local[:, left : left + 512]
                value = jnp.tanh(logits[here] * gain + shift) * half + jnp.where(match, -half, half)
                weights[here] = value.astype(BF16)
        w = weights[0:tall, 0:wide]
        add_to(gh, (rows, slice(None)), {("h", s) for s in high_slots}, dot(w, low_block, ((1,), (0,))))
        add_to(gl, (slice(None), cols), {("l", s) for s in low_slots}, dot(high_block, w, ((0,), (0,))))

    def take_part(slots):
        for dx, dy in slots:
            prow[:, low_cols((dx, dy))] = part[dy, dx]

    pairs = [[(dz, 0), (dz, 1)] for dz in (0, 1, 7, 2, 6, 3, 5, 4)]
    h_one, h_two, h_far = sum(pairs[:3], []), sum(pairs[3:5], []), sum(pairs[5:], [])

    for dz in (0, 1, 7):
        high_other[dz].wait_recv()
    low_a[1, 1].wait_recv()
    low_b[1, 1].wait_recv()
    for e in (1, 2, 3):
        part_y[e].wait_recv()
    take_part(NEAR + FAR)
    block(NEAR, h_one)
    for dz in (3, 5):
        high_same[dz].wait_recv()
        to_other_core(dz)
    for dz in (2, 6):
        high_other[dz].wait_recv()
    four_a.wait_recv()
    four_b.wait_recv()
    to_other_core(4)
    block(NEAR, h_two)
    for dz in (3, 5, 4):
        high_other[dz].wait_recv()
    block(NEAR, h_far)

    a_first, b_first, a_next, b_next = {}, {}, {}, {}

    def low_first(d, e):
        encode(ship_a.at[e, d], gl[a_rows, low_cols((d, e))])
        a_first[4 - e, d] = send(ship_a.at[e, d], got_a.at[4 - e, d], dy=e)
        encode(ship_b.at[e, d], gl[b_rows, low_cols((e, d))])
        b_first[4 - e, d] = send(ship_b.at[e, d], got_b.at[4 - e, d], dx=e)

    for e in (1, 3, 2):
        low_first(0, e)
    low_first(1, 1)
    for slot in FAR:
        low_a[slot].wait_recv()
        low_b[slot].wait_recv()
    block(FAR, h_far)

    from_core = {}

    def core_sum_send(dz):
        from_core[dz] = send(gh.at[high_rows(dz, 1)], got_core.at[dz], dc=1)

    def core_sum_take(dz):
        from_core[dz].wait_recv()
        gh[high_rows(dz, 0), :] += got_core[dz]

    for dz in (4, 3, 5):
        core_sum_send(dz)
    block(FAR[:4], h_one + h_two)
    core_sum_take(4)
    encode(ship_four.at[0], gh[high_rows(4, 0, 0, 64), :])
    encode(ship_four.at[1], gh[high_rows(4, 0, 64, 64), :])
    four_a = send(ship_four.at[0], got_four.at[0], dz=2)
    four_b = send(ship_four.at[1], got_four.at[1], dz=6)
    core_sum_take(3)
    core_sum_take(5)
    encode(ship_three.at[0], gh[high_rows(3, 0), :])
    encode(ship_three.at[1], gh[high_rows(5, 0), :])
    three_a = send(ship_three.at[0], got_three.at[0], dz=1)
    three_b = send(ship_three.at[1], got_three.at[1], dz=7)
    block(FAR[4:], h_one + h_two)
    for dz in (2, 6, 1, 7, 0):
        core_sum_send(dz)
    for d, e in ((1, 3), (3, 1), (3, 3), (2, 1), (1, 2), (2, 3), (3, 2), (2, 2)):
        low_first(d, e)

    for dz, i, three, four, first, to in ((2, 0, three_a, four_a, 0, 2), (6, 1, three_b, four_b, 64, 6)):
        core_sum_take(dz)
        three.wait_recv()
        four.wait_recv()
        gh[high_rows(dz, 0), :] += decode(got_three.at[i])
        gh[high_rows(dz, 0, first, 64), :] += decode(got_four.at[i])
        encode(ship_two.at[i], gh[high_rows(dz, 0), :])
        two = send(ship_two.at[i], got_two.at[i], dz=to)
        two_a, two_b = (two, None) if i == 0 else (two_a, two)
    core_sum_take(1)
    core_sum_take(7)
    encode(ship_one.at[0], gh[high_rows(1, 0), :])
    one_a = send(ship_one.at[0], got_one.at[0], dz=1)
    encode(ship_one.at[1], gh[high_rows(7, 0), :])
    one_b = send(ship_one.at[1], got_one.at[1], dz=7)

    for d in (1, 3, 2):
        for e in (1, 3, 2):
            a_first[e, d].wait_recv()
        total = gl[a_rows, low_cols((d, 0))]
        for e in (1, 2, 3):
            total += decode(got_a.at[e, d])
        encode(next_a.at[d], total)
        a_next[d] = send(next_a.at[d], last_a.at[d], dx=d)
        for e in (1, 3, 2):
            b_first[e, d].wait_recv()
        total = gl[b_rows, low_cols((0, d))]
        for e in (1, 2, 3):
            total += decode(got_b.at[e, d])
        encode(next_b.at[d], total)
        b_next[d] = send(next_b.at[d], last_b.at[d], dy=d)

    core_sum_take(0)
    for copy in (one_a, one_b, two_a, two_b):
        copy.wait_recv()
    total = gh[high_rows(0, 0), :] + decode(got_one.at[0]) + decode(got_one.at[1])
    high_out[...] = total + decode(got_two.at[0]) + decode(got_two.at[1])
    total_a, total_b = gl[a_rows, low_cols((0, 0))], gl[b_rows, low_cols((0, 0))]
    for e in (1, 3, 2):
        a_first[e, 0].wait_recv()
        b_first[e, 0].wait_recv()
        total_a += decode(got_a.at[e, 0])
        total_b += decode(got_b.at[e, 0])
    for d in (1, 3, 2):
        a_next[d].wait_recv()
        b_next[d].wait_recv()
        total_a += decode(last_a.at[d])
        total_b += decode(last_b.at[d])
    low_out[...] = jnp.concatenate([total_a, total_b], axis=0).T
    for copy in copies:
        copy.wait_send()


def per_device(embed_low, embed_high, partner, log_scale, bias):
    hbm, vmem, smem = (pl.BlockSpec(memory_space=m) for m in (pl.ANY, pltpu.VMEM, pltpu.SMEM))
    group = 16 * ROWS
    grad = jax.ShapeDtypeStruct((ROWS, WIDTH), F32)
    low_piece, high_piece = (HALF + TAIL, ROWS), (ROWS + TAIL, WIDTH)

    def short(*shape):
        return pltpu.VMEM(shape, jnp.int16)

    return pl.pallas_call(
        kernel,
        out_shape=(grad, grad),
        in_specs=[hbm, hbm, hbm, smem, smem],
        out_specs=(vmem, vmem),
        scratch_shapes=[
            pltpu.VMEM((group, WIDTH), BF16),
            pltpu.VMEM((group, WIDTH), BF16),
            pltpu.VMEM((4, 4, 1, ROWS), jnp.int32),
            pltpu.VMEM((1, group), jnp.int32),
            pltpu.VMEM((10 * ROWS, 8 * ROWS), BF16),
            pltpu.VMEM((WIDTH, group), F32),
            pltpu.VMEM((group, WIDTH), F32),
            short(4, 4, *low_piece),
            short(4, 4, *low_piece),
            short(4, 4, *low_piece),
            short(4, 4, *low_piece),
            short(4, *low_piece),
            short(4, *low_piece),
            short(4, *low_piece),
            short(4, *low_piece),
            pltpu.VMEM((8, ROWS, WIDTH), F32),
            short(2, *high_piece),
            short(2, ROWS // 2 + TAIL, WIDTH),
            short(2, *high_piece),
            short(2, *high_piece),
            short(2, *high_piece),
            short(2, ROWS // 2 + TAIL, WIDTH),
            short(2, *high_piece),
            short(2, *high_piece),
            pltpu.SemaphoreType.DMA((3,)),
            pltpu.SemaphoreType.DMA((96,)),
            pltpu.SemaphoreType.DMA((96,)),
        ],
        compiler_params=pltpu.CompilerParams(
            collective_id=0, has_side_effects=True, vmem_limit_bytes=56 * 2**20
        ),
    )(embed_low, embed_high, partner.reshape(1, ROWS), log_scale.reshape(1, 1), bias.reshape(1, 1))


def solution(mesh):
    in_specs = (
        P(("blk", "narrow"), None),
        P(("blk", "narrow"), None),
        P(("blk", "narrow")),
        P(),
        P(),
    )
    out_specs = (P(("blk", "narrow"), None), P(("blk", "narrow"), None))
    return jax.shard_map(
        per_device, mesh=mesh, in_specs=in_specs, out_specs=out_specs, check_vma=False
    )
```

```python
import functools

import jax
import jax.numpy as jnp
from jax import lax
from jax.experimental import pallas as pl
from jax.experimental.pallas import tpu as pltpu
from jax.sharding import PartitionSpec as P

MESH = pl.DeviceIdType.MESH
F32, BF16 = jnp.float32, jnp.bfloat16
X, Y, Z = 4, 4, 8
ROWS, WIDTH = 128, 384
HALF = WIDTH // 2

NEAR = [(0, 0), (1, 0), (3, 0), (0, 1), (0, 3), (2, 0), (0, 2), (1, 1)]
FAR = [(3, 3), (1, 3), (3, 1), (2, 1), (1, 2), (2, 3), (3, 2), (2, 2)]
LOW_AT = {slot: i for i, slot in enumerate(NEAR + FAR)}
HIGH_NEAR = [(0, 0), (0, 1), (1, 0), (7, 0), (1, 1), (7, 1), (6, 0), (2, 0), (6, 1), (2, 1)]
HIGH_FAR = [(4, 0), (4, 1), (3, 0), (3, 1), (5, 0), (5, 1)]
HIGH_AT = {slot: i for i, slot in enumerate(HIGH_NEAR + HIGH_FAR)}
TAIL = 16
STEPS = 32767.0


def dot(a, b, over):
    return lax.dot_general(a, b, (over, ((), ())), preferred_element_type=F32)


def encode(ref, value):
    rows = value.shape[0]
    top = jnp.maximum(jnp.max(jnp.abs(value), axis=0, keepdims=True), 1e-30)
    exponent = jnp.ceil(jnp.log2(top))
    ref[0:rows, :] = jnp.round(value * (STEPS * jnp.exp2(-exponent))).astype(jnp.int32).astype(jnp.int16)
    ref[rows : rows + TAIL, :] = jnp.broadcast_to(exponent, (TAIL, value.shape[1])).astype(jnp.int32).astype(jnp.int16)


def decode(ref):
    rows = ref.shape[0] - TAIL
    exponent = ref[rows : rows + TAIL, :].astype(jnp.int32).astype(F32)[0:1]
    return ref[0:rows, :].astype(jnp.int32).astype(F32) * (jnp.exp2(exponent) * (1.0 / STEPS))


def kernel(
    low_in, high_in, partner_in, log_scale, bias_in,
    low_out, high_out,
    low, high, part, prow, weights, gl, gh,
    ship_a, ship_b, got_a, got_b, next_a, next_b, last_a, last_b,
    got_core, ship_three, ship_four, ship_two, ship_one, got_three, got_four, got_two, got_one,
    load_sems, send_sems, recv_sems,
):
    blk, narrow = lax.axis_index("blk"), lax.axis_index("narrow")
    x, z, y, core = blk // 16, (blk // 2) % 8, (narrow // 2) * 2 + blk % 2, narrow % 2

    def device(dx=0, dy=0, dz=0, dc=0):
        px, py, pz, pc = (x + dx) % X, (y + dy) % Y, (z + dz) % Z, (core + dc) % 2
        return ((px * Z + pz) * 2 + py % 2, (py // 2) * 2 + pc)

    copies = []

    def send(src, dst, **to):
        k = len(copies)
        copy = pltpu.make_async_remote_copy(
            src, dst, send_sems.at[k], recv_sems.at[k], device_id=device(**to), device_id_type=MESH
        )
        copy.start()
        copies.append(copy)
        return copy

    def low_rows(slot, first=0, count=ROWS):
        return pl.ds(LOW_AT[slot] * ROWS + first, count)

    def low_cols(slot):
        return pl.ds(LOW_AT[slot] * ROWS, ROWS)

    def high_rows(dz, dc, first=0, count=ROWS):
        return pl.ds(HIGH_AT[dz, dc] * ROWS + first, count)

    def high_cols(dz, dc):
        return pl.ds(HIGH_AT[dz, dc] * ROWS, ROWS)

    a_rows, b_rows = pl.ds(0, HALF), pl.ds(HALF, HALF)
    own_low, own_high = low.at[low_rows((0, 0))], high.at[high_rows(0, 0)]
    loads = [(low_in, own_low), (high_in, own_high), (partner_in, part.at[0, 0])]
    loads = [pltpu.make_async_copy(src, dst, load_sems.at[i]) for i, (src, dst) in enumerate(loads)]
    for load in loads:
        load.start()

    peers = [dict(dx=e) for e in (1, 2, 3)] + [dict(dy=e) for e in (1, 2, 3)]
    peers += [dict(dz=e) for e in (1, 2, 6, 7)] + [dict(dc=1)]
    barrier = pltpu.get_barrier_semaphore()
    for peer in peers:
        pl.semaphore_signal(barrier, inc=1, device_id=device(**peer), device_id_type=MESH)
    for load in loads:
        load.wait()
    scale = jnp.exp(jnp.full((1, 512), log_scale[0, 0], F32))
    gain, shift, half = 0.5 * scale, 0.5 * bias_in[0, 0], 0.5 * scale
    pl.semaphore_wait(barrier, len(peers))

    low_x, low_y, low_a, low_b, part_x, part_y, high_same, high_other = {}, {}, {}, {}, {}, {}, {}, {}
    for e in (1, 3, 2):
        part_x[4 - e] = send(part.at[0, 0], part.at[0, 4 - e], dx=e)
    for e in (1, 3):
        low_x[4 - e] = send(own_low, low.at[low_rows((4 - e, 0))], dx=e)
        low_y[4 - e] = send(own_low, low.at[low_rows((0, 4 - e))], dy=e)
    for e in (2, 6):
        high_same[8 - e] = send(own_high, high.at[high_rows(8 - e, 0)], dz=e)
    low_x[2] = send(own_low, low.at[low_rows((2, 0))], dx=2)
    low_y[2] = send(own_low, low.at[low_rows((0, 2))], dy=2)
    for e in (1, 7):
        high_same[8 - e] = send(own_high, high.at[high_rows(8 - e, 0)], dz=e)
    high_other[0] = send(own_high, high.at[high_rows(0, 1)], dc=1)

    def to_other_core(dz):
        rows = high_rows(dz, 0)
        high_other[dz] = send(high.at[rows], high.at[high_rows(dz, 1)], dc=1)

    def pass_low(d):
        low_x[d].wait_recv()
        for e in (1, 3, 2):
            src = low.at[low_rows((d, 0), 0, 64)]
            low_a[d, 4 - e] = send(src, low.at[low_rows((d, 4 - e), 0, 64)], dy=e)
        low_y[d].wait_recv()
        for e in (1, 3, 2):
            src = low.at[low_rows((0, d), 64, 64)]
            low_b[4 - e, d] = send(src, low.at[low_rows((4 - e, d), 64, 64)], dx=e)

    for e in (1, 3, 2):
        part_x[e].wait_recv()
    for e in (1, 3, 2):
        part_y[4 - e] = send(part.at[0], part.at[4 - e], dy=e)
    pass_low(1)
    pass_low(3)
    pass_low(2)
    high_same[6].wait_recv()
    high_same[5] = send(high.at[high_rows(6, 0)], high.at[high_rows(5, 0)], dz=1)
    four_a = send(high.at[high_rows(6, 0, 0, 64)], high.at[high_rows(4, 0, 0, 64)], dz=2)
    high_same[2].wait_recv()
    high_same[3] = send(high.at[high_rows(2, 0)], high.at[high_rows(3, 0)], dz=7)
    four_b = send(high.at[high_rows(2, 0, 64, 64)], high.at[high_rows(4, 0, 64, 64)], dz=6)
    for dz in (1, 7):
        high_same[dz].wait_recv()
        to_other_core(dz)
    to_other_core(6)
    to_other_core(2)

    started = set()

    def add_to(ref, index, keys, value):
        if keys <= started:
            ref[index] += value
        else:
            ref[index] = value
            started.update(keys)

    def block(low_slots, high_slots):
        first_low, first_high = LOW_AT[low_slots[0]], HIGH_AT[high_slots[0]]
        wide, tall = len(low_slots) * ROWS, len(high_slots) * ROWS
        cols, rows = pl.ds(first_low * ROWS, wide), pl.ds(first_high * ROWS, tall)
        low_block, high_block = low[cols, :], high[rows, :]
        logits = dot(high_block, low_block, ((1,), (1,)))
        wanted = prow[:, cols]
        for i, (dz, dc) in enumerate(high_slots):
            b, n = device(dz=dz, dc=dc)
            local = wanted - (b * 4 + n) * ROWS
            ids = lax.broadcasted_iota(jnp.int32, (ROWS, 512), 0)
            for left in range(0, wide, 512):
                here = (slice(i * ROWS, (i + 1) * ROWS), slice(left, left + 512))
                match = ids == local[:, left : left + 512]
                value = jnp.tanh(logits[here] * gain + shift) * half + jnp.where(match, -half, half)
                weights[here] = value.astype(BF16)
        w = weights[0:tall, 0:wide]
        add_to(gh, (slice(None), rows), {("h", s) for s in high_slots}, dot(low_block, w, ((0,), (1,))))
        add_to(gl, (slice(None), cols), {("l", s) for s in low_slots}, dot(high_block, w, ((0,), (0,))))

    def take_part(slots):
        for dx, dy in slots:
            prow[:, low_cols((dx, dy))] = part[dy, dx]

    a_first, b_first, a_next, b_next = {}, {}, {}, {}

    def low_first(slots):
        for dx, dy in slots:
            if dy:
                encode(ship_a.at[dy, dx], gl[a_rows, low_cols((dx, dy))])
            if dx:
                encode(ship_b.at[dx, dy], gl[b_rows, low_cols((dx, dy))])
        for dx, dy in slots:
            if dy:
                a_first[4 - dy, dx] = send(ship_a.at[dy, dx], got_a.at[4 - dy, dx], dy=dy)
            if dx:
                b_first[4 - dx, dy] = send(ship_b.at[dx, dy], got_b.at[4 - dx, dy], dx=dx)

    from_core = {}

    def core_sum_send(dz):
        from_core[dz] = send(gh.at[:, high_cols(dz, 1)], got_core.at[dz], dc=1)

    def core_sum_take(dz):
        from_core[dz].wait_recv()
        gh[:, high_cols(dz, 0)] += got_core[dz]

    low_a[1, 1].wait_recv()
    low_b[1, 1].wait_recv()
    for e in (1, 2, 3):
        part_y[e].wait_recv()
    take_part(NEAR + FAR)
    high_other[0].wait_recv()
    block(NEAR, HIGH_NEAR[:4])
    for dz in (1, 7, 6, 2):
        high_other[dz].wait_recv()
    block(NEAR, HIGH_NEAR[4:])
    for slot in FAR[:4]:
        low_a[slot].wait_recv()
        low_b[slot].wait_recv()
    block(FAR[:4], HIGH_NEAR[:4])
    for dz in (3, 5):
        high_same[dz].wait_recv()
        to_other_core(dz)
    four_a.wait_recv()
    four_b.wait_recv()
    to_other_core(4)
    block(FAR[:4], HIGH_NEAR[4:])
    for slot in FAR[4:]:
        low_a[slot].wait_recv()
        low_b[slot].wait_recv()
    block(FAR[4:], HIGH_NEAR[:6])
    for dz in (1, 7, 0):
        core_sum_send(dz)
    high_other[4].wait_recv()
    high_other[3].wait_recv()
    block(NEAR, HIGH_FAR[:4])
    core_sum_take(1)
    core_sum_take(7)
    encode(ship_one.at[0], gh[:, high_cols(1, 0)])
    encode(ship_one.at[1], gh[:, high_cols(7, 0)])
    one_a = send(ship_one.at[0], got_one.at[0], dz=1)
    one_b = send(ship_one.at[1], got_one.at[1], dz=7)
    block(FAR, HIGH_FAR[:4])
    core_sum_send(4)
    core_sum_send(3)
    high_other[5].wait_recv()
    block(FAR[:4], HIGH_FAR[4:])
    low_first(FAR[:4])
    block(NEAR, HIGH_FAR[4:])
    core_sum_take(4)
    core_sum_take(3)
    encode(ship_four.at[0], gh[a_rows, high_cols(4, 0)])
    encode(ship_four.at[1], gh[b_rows, high_cols(4, 0)])
    encode(ship_three.at[0], gh[:, high_cols(3, 0)])
    four_a = send(ship_four.at[0], got_four.at[0], dz=2)
    four_b = send(ship_four.at[1], got_four.at[1], dz=6)
    three_a = send(ship_three.at[0], got_three.at[0], dz=1)
    low_first(NEAR)
    block(FAR[4:], HIGH_FAR[4:])
    core_sum_send(5)
    block(FAR[4:], HIGH_NEAR[6:])
    core_sum_send(6)
    core_sum_send(2)
    low_first(FAR[4:])
    core_sum_take(5)
    encode(ship_three.at[1], gh[:, high_cols(5, 0)])
    three_b = send(ship_three.at[1], got_three.at[1], dz=7)

    core_sum_take(2)
    core_sum_take(6)
    three_a.wait_recv()
    four_a.wait_recv()
    gh[:, high_cols(2, 0)] += decode(got_three.at[0])
    gh[a_rows, high_cols(2, 0)] += decode(got_four.at[0])
    encode(ship_two.at[0], gh[:, high_cols(2, 0)])
    two_a = send(ship_two.at[0], got_two.at[0], dz=2)
    three_b.wait_recv()
    four_b.wait_recv()
    gh[:, high_cols(6, 0)] += decode(got_three.at[1])
    gh[b_rows, high_cols(6, 0)] += decode(got_four.at[1])
    encode(ship_two.at[1], gh[:, high_cols(6, 0)])
    two_b = send(ship_two.at[1], got_two.at[1], dz=6)
    for d in (1, 3, 2):
        for e in (1, 3, 2):
            a_first[e, d].wait_recv()
        total = gl[a_rows, low_cols((d, 0))]
        for e in (1, 2, 3):
            total += decode(got_a.at[e, d])
        encode(next_a.at[d], total)
        a_next[d] = send(next_a.at[d], last_a.at[d], dx=d)
        for e in (1, 3, 2):
            b_first[e, d].wait_recv()
        total = gl[b_rows, low_cols((0, d))]
        for e in (1, 2, 3):
            total += decode(got_b.at[e, d])
        encode(next_b.at[d], total)
        b_next[d] = send(next_b.at[d], last_b.at[d], dy=d)

    core_sum_take(0)
    for copy in (one_a, one_b, two_a, two_b):
        copy.wait_recv()
    total = gh[:, high_cols(0, 0)] + decode(got_one.at[0]) + decode(got_one.at[1])
    high_out[...] = (total + decode(got_two.at[0]) + decode(got_two.at[1])).T
    total_a, total_b = gl[a_rows, low_cols((0, 0))], gl[b_rows, low_cols((0, 0))]
    for e in (1, 3, 2):
        a_first[e, 0].wait_recv()
        b_first[e, 0].wait_recv()
        total_a += decode(got_a.at[e, 0])
        total_b += decode(got_b.at[e, 0])
    for d in (1, 3, 2):
        a_next[d].wait_recv()
        b_next[d].wait_recv()
        total_a += decode(last_a.at[d])
        total_b += decode(last_b.at[d])
    low_out[...] = jnp.concatenate([total_a, total_b], axis=0).T
    for copy in copies:
        copy.wait_send()


def per_device(embed_low, embed_high, partner, log_scale, bias):
    hbm, vmem, smem = (pl.BlockSpec(memory_space=m) for m in (pl.ANY, pltpu.VMEM, pltpu.SMEM))
    group = 16 * ROWS
    grad = jax.ShapeDtypeStruct((ROWS, WIDTH), F32)
    half_piece, piece = (HALF + TAIL, ROWS), (WIDTH + TAIL, ROWS)

    def short(*shape):
        return pltpu.VMEM(shape, jnp.int16)

    return pl.pallas_call(
        kernel,
        out_shape=(grad, grad),
        in_specs=[hbm, hbm, hbm, smem, smem],
        out_specs=(vmem, vmem),
        scratch_shapes=[
            pltpu.VMEM((group, WIDTH), BF16),
            pltpu.VMEM((group, WIDTH), BF16),
            pltpu.VMEM((4, 4, 1, ROWS), jnp.int32),
            pltpu.VMEM((1, group), jnp.int32),
            pltpu.VMEM((8 * ROWS, 8 * ROWS), BF16),
            pltpu.VMEM((WIDTH, group), F32),
            pltpu.VMEM((WIDTH, group), F32),
            short(4, 4, *half_piece),
            short(4, 4, *half_piece),
            short(4, 4, *half_piece),
            short(4, 4, *half_piece),
            short(4, *half_piece),
            short(4, *half_piece),
            short(4, *half_piece),
            short(4, *half_piece),
            pltpu.VMEM((8, WIDTH, ROWS), F32),
            short(2, *piece),
            short(2, *half_piece),
            short(2, *piece),
            short(2, *piece),
            short(2, *piece),
            short(2, *half_piece),
            short(2, *piece),
            short(2, *piece),
            pltpu.SemaphoreType.DMA((3,)),
            pltpu.SemaphoreType.DMA((96,)),
            pltpu.SemaphoreType.DMA((96,)),
        ],
        compiler_params=pltpu.CompilerParams(
            collective_id=0, has_side_effects=True, vmem_limit_bytes=56 * 2**20
        ),
    )(embed_low, embed_high, partner.reshape(1, ROWS), log_scale.reshape(1, 1), bias.reshape(1, 1))


def solution(mesh):
    in_specs = (
        P(("blk", "narrow"), None),
        P(("blk", "narrow"), None),
        P(("blk", "narrow")),
        P(),
        P(),
    )
    out_specs = (P(("blk", "narrow"), None), P(("blk", "narrow"), None))
    return jax.shard_map(
        per_device, mesh=mesh, in_specs=in_specs, out_specs=out_specs, check_vma=False
    )
```

```python
import functools

import jax
import jax.numpy as jnp
from jax import lax
from jax.experimental import pallas as pl
from jax.experimental.pallas import tpu as pltpu
from jax.sharding import PartitionSpec as P

MESH = pl.DeviceIdType.MESH
F32, BF16 = jnp.float32, jnp.bfloat16
X, Y, Z = 4, 4, 8
ROWS, WIDTH = 128, 384
HALF = WIDTH // 2

NEAR = [(0, 0), (1, 0), (3, 0), (0, 1), (0, 3), (2, 0), (0, 2), (1, 1)]
FAR = [(3, 3), (1, 3), (3, 1), (2, 1), (1, 2), (2, 3), (3, 2), (2, 2)]
LOW_AT = {slot: i for i, slot in enumerate(NEAR + FAR)}
HIGH_NEAR = [(0, 0), (0, 1), (1, 0), (7, 0), (1, 1), (7, 1), (6, 0), (2, 0), (6, 1), (2, 1)]
HIGH_FAR = [(4, 0), (4, 1), (3, 0), (3, 1), (5, 0), (5, 1)]
HIGH_AT = {slot: i for i, slot in enumerate(HIGH_NEAR + HIGH_FAR)}
TAIL = 16
STEPS = 32767.0


def dot(a, b, over):
    return lax.dot_general(a, b, (over, ((), ())), preferred_element_type=F32)


def encode(ref, value):
    rows = value.shape[0]
    top = jnp.maximum(jnp.max(jnp.abs(value), axis=0, keepdims=True), 1e-30)
    exponent = jnp.ceil(jnp.log2(top))
    ref[0:rows, :] = jnp.round(value * (STEPS * jnp.exp2(-exponent))).astype(jnp.int32).astype(jnp.int16)
    ref[rows : rows + TAIL, :] = jnp.broadcast_to(exponent, (TAIL, value.shape[1])).astype(jnp.int32).astype(jnp.int16)


def decode(ref):
    rows = ref.shape[0] - TAIL
    exponent = ref[rows : rows + TAIL, :].astype(jnp.int32).astype(F32)[0:1]
    return ref[0:rows, :].astype(jnp.int32).astype(F32) * (jnp.exp2(exponent) * (1.0 / STEPS))


def kernel(
    low_in, high_in, partner_in, log_scale, bias_in,
    out,
    low, high, part, prow, weights, gl, gh,
    ship_a, ship_b, got_a, got_b, next_a, next_b, last_a, last_b,
    got_core, ship_three, ship_four, ship_two, ship_one, got_three, got_four, got_two, got_one,
    load_sems, send_sems, recv_sems,
):
    blk, narrow = lax.axis_index("blk"), lax.axis_index("narrow")
    x, z, y, core = blk // 16, (blk // 2) % 8, (narrow // 2) * 2 + blk % 2, narrow % 2

    def device(dx=0, dy=0, dz=0, dc=0):
        px, py, pz, pc = (x + dx) % X, (y + dy) % Y, (z + dz) % Z, (core + dc) % 2
        return ((px * Z + pz) * 2 + py % 2, (py // 2) * 2 + pc)

    copies = []

    def send(src, dst, **to):
        k = len(copies)
        copy = pltpu.make_async_remote_copy(
            src, dst, send_sems.at[k], recv_sems.at[k], device_id=device(**to), device_id_type=MESH
        )
        copy.start()
        copies.append(copy)
        return copy

    def low_rows(slot, first=0, count=ROWS):
        return pl.ds(LOW_AT[slot] * ROWS + first, count)

    def low_cols(slot):
        return pl.ds(LOW_AT[slot] * ROWS, ROWS)

    def high_rows(dz, dc, first=0, count=ROWS):
        return pl.ds(HIGH_AT[dz, dc] * ROWS + first, count)

    def high_cols(dz, dc):
        return pl.ds(HIGH_AT[dz, dc] * ROWS, ROWS)

    a_rows, b_rows = pl.ds(0, HALF), pl.ds(HALF, HALF)
    own_low, own_high = low.at[low_rows((0, 0))], high.at[high_rows(0, 0)]
    loads = [(low_in, own_low), (high_in, own_high), (partner_in, part.at[0, 0])]
    loads = [pltpu.make_async_copy(src, dst, load_sems.at[i]) for i, (src, dst) in enumerate(loads)]
    for load in loads:
        load.start()

    peers = [dict(dx=e) for e in (1, 2, 3)] + [dict(dy=e) for e in (1, 2, 3)]
    peers += [dict(dz=e) for e in (1, 2, 6, 7)] + [dict(dc=1)]
    barrier = pltpu.get_barrier_semaphore()
    for peer in peers:
        pl.semaphore_signal(barrier, inc=1, device_id=device(**peer), device_id_type=MESH)
    for load in loads:
        load.wait()
    scale = jnp.exp(jnp.full((1, 512), log_scale[0, 0], F32))
    gain, shift, half = 0.5 * scale, 0.5 * bias_in[0, 0], 0.5 * scale
    pl.semaphore_wait(barrier, len(peers))

    low_x, low_y, low_a, low_b, part_x, part_y, high_same, high_other = {}, {}, {}, {}, {}, {}, {}, {}
    for e in (1, 3, 2):
        part_x[4 - e] = send(part.at[0, 0], part.at[0, 4 - e], dx=e)
    for e in (1, 3):
        low_x[4 - e] = send(own_low, low.at[low_rows((4 - e, 0))], dx=e)
        low_y[4 - e] = send(own_low, low.at[low_rows((0, 4 - e))], dy=e)
    for e in (2, 6):
        high_same[8 - e] = send(own_high, high.at[high_rows(8 - e, 0)], dz=e)
    low_x[2] = send(own_low, low.at[low_rows((2, 0))], dx=2)
    low_y[2] = send(own_low, low.at[low_rows((0, 2))], dy=2)
    for e in (1, 7):
        high_same[8 - e] = send(own_high, high.at[high_rows(8 - e, 0)], dz=e)
    high_other[0] = send(own_high, high.at[high_rows(0, 1)], dc=1)

    def to_other_core(dz):
        rows = high_rows(dz, 0)
        high_other[dz] = send(high.at[rows], high.at[high_rows(dz, 1)], dc=1)

    def pass_low(d):
        low_x[d].wait_recv()
        for e in (1, 3, 2):
            src = low.at[low_rows((d, 0), 0, 64)]
            low_a[d, 4 - e] = send(src, low.at[low_rows((d, 4 - e), 0, 64)], dy=e)
        low_y[d].wait_recv()
        for e in (1, 3, 2):
            src = low.at[low_rows((0, d), 64, 64)]
            low_b[4 - e, d] = send(src, low.at[low_rows((4 - e, d), 64, 64)], dx=e)

    for e in (1, 3, 2):
        part_x[e].wait_recv()
    for e in (1, 3, 2):
        part_y[4 - e] = send(part.at[0], part.at[4 - e], dy=e)
    pass_low(1)
    pass_low(3)
    pass_low(2)
    high_same[6].wait_recv()
    high_same[5] = send(high.at[high_rows(6, 0)], high.at[high_rows(5, 0)], dz=1)
    four_a = send(high.at[high_rows(6, 0, 0, 64)], high.at[high_rows(4, 0, 0, 64)], dz=2)
    high_same[2].wait_recv()
    high_same[3] = send(high.at[high_rows(2, 0)], high.at[high_rows(3, 0)], dz=7)
    four_b = send(high.at[high_rows(2, 0, 64, 64)], high.at[high_rows(4, 0, 64, 64)], dz=6)
    for dz in (1, 7):
        high_same[dz].wait_recv()
        to_other_core(dz)
    to_other_core(6)
    to_other_core(2)

    started = set()

    def add_to(ref, index, keys, value):
        if keys <= started:
            ref[index] += value
        else:
            ref[index] = value
            started.update(keys)

    def block(low_slots, high_slots):
        first_low, first_high = LOW_AT[low_slots[0]], HIGH_AT[high_slots[0]]
        wide, tall = len(low_slots) * ROWS, len(high_slots) * ROWS
        cols, rows = pl.ds(first_low * ROWS, wide), pl.ds(first_high * ROWS, tall)
        low_block, high_block = low[cols, :], high[rows, :]
        logits = dot(high_block, low_block, ((1,), (1,)))
        wanted = prow[:, cols]
        for i, (dz, dc) in enumerate(high_slots):
            b, n = device(dz=dz, dc=dc)
            local = wanted - (b * 4 + n) * ROWS
            ids = lax.broadcasted_iota(jnp.int32, (ROWS, 512), 0)
            for left in range(0, wide, 512):
                here = (slice(i * ROWS, (i + 1) * ROWS), slice(left, left + 512))
                match = ids == local[:, left : left + 512]
                value = jnp.tanh(logits[here] * gain + shift) * half + jnp.where(match, -half, half)
                weights[here] = value.astype(BF16)
        w = weights[0:tall, 0:wide]
        add_to(gh, (slice(None), rows), {("h", s) for s in high_slots}, dot(low_block, w, ((0,), (1,))))
        add_to(gl, (slice(None), cols), {("l", s) for s in low_slots}, dot(high_block, w, ((0,), (0,))))

    def take_part(slots):
        for dx, dy in slots:
            prow[:, low_cols((dx, dy))] = part[dy, dx]

    a_first, b_first, a_next, b_next = {}, {}, {}, {}

    def low_first(slots):
        for dx, dy in slots:
            if dy:
                encode(ship_a.at[dy, dx], gl[a_rows, low_cols((dx, dy))])
            if dx:
                encode(ship_b.at[dx, dy], gl[b_rows, low_cols((dx, dy))])
        for dx, dy in slots:
            if dy:
                a_first[4 - dy, dx] = send(ship_a.at[dy, dx], got_a.at[4 - dy, dx], dy=dy)
            if dx:
                b_first[4 - dx, dy] = send(ship_b.at[dx, dy], got_b.at[4 - dx, dy], dx=dx)

    from_core = {}

    def core_sum_send(dz):
        from_core[dz] = send(gh.at[:, high_cols(dz, 1)], got_core.at[dz], dc=1)

    def core_sum_take(dz):
        from_core[dz].wait_recv()
        gh[:, high_cols(dz, 0)] += got_core[dz]

    low_a[1, 1].wait_recv()
    low_b[1, 1].wait_recv()
    for e in (1, 2, 3):
        part_y[e].wait_recv()
    take_part(NEAR + FAR)
    high_other[0].wait_recv()
    block(NEAR, HIGH_NEAR[:4])
    for dz in (1, 7, 6, 2):
        high_other[dz].wait_recv()
    block(NEAR, HIGH_NEAR[4:])
    for slot in FAR[:4]:
        low_a[slot].wait_recv()
        low_b[slot].wait_recv()
    block(FAR[:4], HIGH_NEAR[:4])
    for dz in (3, 5):
        high_same[dz].wait_recv()
        to_other_core(dz)
    four_a.wait_recv()
    four_b.wait_recv()
    to_other_core(4)
    block(FAR[:4], HIGH_NEAR[4:])
    for slot in FAR[4:]:
        low_a[slot].wait_recv()
        low_b[slot].wait_recv()
    block(FAR[4:], HIGH_NEAR[:6])
    for dz in (1, 7, 0):
        core_sum_send(dz)
    high_other[4].wait_recv()
    high_other[3].wait_recv()
    block(NEAR, HIGH_FAR[:4])
    core_sum_take(1)
    core_sum_take(7)
    encode(ship_one.at[0], gh[:, high_cols(1, 0)])
    encode(ship_one.at[1], gh[:, high_cols(7, 0)])
    one_a = send(ship_one.at[0], got_one.at[0], dz=1)
    one_b = send(ship_one.at[1], got_one.at[1], dz=7)
    block(FAR, HIGH_FAR[:4])
    core_sum_send(4)
    core_sum_send(3)
    high_other[5].wait_recv()
    block(FAR[:4], HIGH_FAR[4:])
    low_first(FAR[:4])
    block(NEAR, HIGH_FAR[4:])
    core_sum_take(4)
    core_sum_take(3)
    encode(ship_four.at[0], gh[a_rows, high_cols(4, 0)])
    encode(ship_four.at[1], gh[b_rows, high_cols(4, 0)])
    encode(ship_three.at[0], gh[:, high_cols(3, 0)])
    four_a = send(ship_four.at[0], got_four.at[0], dz=2)
    four_b = send(ship_four.at[1], got_four.at[1], dz=6)
    three_a = send(ship_three.at[0], got_three.at[0], dz=1)
    low_first(NEAR)
    block(FAR[4:], HIGH_FAR[4:])
    core_sum_send(5)
    block(FAR[4:], HIGH_NEAR[6:])
    core_sum_send(6)
    core_sum_send(2)
    low_first(FAR[4:])
    core_sum_take(5)
    encode(ship_three.at[1], gh[:, high_cols(5, 0)])
    three_b = send(ship_three.at[1], got_three.at[1], dz=7)

    core_sum_take(2)
    core_sum_take(6)
    three_a.wait_recv()
    four_a.wait_recv()
    gh[:, high_cols(2, 0)] += decode(got_three.at[0])
    gh[a_rows, high_cols(2, 0)] += decode(got_four.at[0])
    encode(ship_two.at[0], gh[:, high_cols(2, 0)])
    two_a = send(ship_two.at[0], got_two.at[0], dz=2)
    three_b.wait_recv()
    four_b.wait_recv()
    gh[:, high_cols(6, 0)] += decode(got_three.at[1])
    gh[b_rows, high_cols(6, 0)] += decode(got_four.at[1])
    encode(ship_two.at[1], gh[:, high_cols(6, 0)])
    two_b = send(ship_two.at[1], got_two.at[1], dz=6)
    for d in (1, 3, 2):
        for e in (1, 3, 2):
            a_first[e, d].wait_recv()
        total = gl[a_rows, low_cols((d, 0))]
        for e in (1, 2, 3):
            total += decode(got_a.at[e, d])
        encode(next_a.at[d], total)
        a_next[d] = send(next_a.at[d], last_a.at[d], dx=d)
        for e in (1, 3, 2):
            b_first[e, d].wait_recv()
        total = gl[b_rows, low_cols((0, d))]
        for e in (1, 2, 3):
            total += decode(got_b.at[e, d])
        encode(next_b.at[d], total)
        b_next[d] = send(next_b.at[d], last_b.at[d], dy=d)

    core_sum_take(0)
    one_a.wait_recv()
    one_b.wait_recv()
    total = gh[:, high_cols(0, 0)] + decode(got_one.at[0]) + decode(got_one.at[1])
    total_a, total_b = gl[a_rows, low_cols((0, 0))], gl[b_rows, low_cols((0, 0))]
    for e in (1, 3, 2):
        a_first[e, 0].wait_recv()
        b_first[e, 0].wait_recv()
        total_a += decode(got_a.at[e, 0])
        total_b += decode(got_b.at[e, 0])
    two_a.wait_recv()
    two_b.wait_recv()
    out[ROWS:, :] = (total + decode(got_two.at[0]) + decode(got_two.at[1])).T
    for d in (1, 3, 2):
        a_next[d].wait_recv()
        b_next[d].wait_recv()
        total_a += decode(last_a.at[d])
        total_b += decode(last_b.at[d])
    out[:ROWS, :] = jnp.concatenate([total_a, total_b], axis=0).T
    for copy in copies:
        copy.wait_send()


def per_device(embed_low, embed_high, partner, log_scale, bias):
    hbm, vmem, smem = (pl.BlockSpec(memory_space=m) for m in (pl.ANY, pltpu.VMEM, pltpu.SMEM))
    group = 16 * ROWS
    grads = jax.ShapeDtypeStruct((2 * ROWS, WIDTH), F32)
    half_piece, piece = (HALF + TAIL, ROWS), (WIDTH + TAIL, ROWS)

    def short(*shape):
        return pltpu.VMEM(shape, jnp.int16)

    grads = pl.pallas_call(
        kernel,
        out_shape=grads,
        in_specs=[hbm, hbm, hbm, smem, smem],
        out_specs=vmem,
        scratch_shapes=[
            pltpu.VMEM((group, WIDTH), BF16),
            pltpu.VMEM((group, WIDTH), BF16),
            pltpu.VMEM((4, 4, 1, ROWS), jnp.int32),
            pltpu.VMEM((1, group), jnp.int32),
            pltpu.VMEM((8 * ROWS, 8 * ROWS), BF16),
            pltpu.VMEM((WIDTH, group), F32),
            pltpu.VMEM((WIDTH, group), F32),
            short(4, 4, *half_piece),
            short(4, 4, *half_piece),
            short(4, 4, *half_piece),
            short(4, 4, *half_piece),
            short(4, *half_piece),
            short(4, *half_piece),
            short(4, *half_piece),
            short(4, *half_piece),
            pltpu.VMEM((8, WIDTH, ROWS), F32),
            short(2, *piece),
            short(2, *half_piece),
            short(2, *piece),
            short(2, *piece),
            short(2, *piece),
            short(2, *half_piece),
            short(2, *piece),
            short(2, *piece),
            pltpu.SemaphoreType.DMA((3,)),
            pltpu.SemaphoreType.DMA((96,)),
            pltpu.SemaphoreType.DMA((96,)),
        ],
        compiler_params=pltpu.CompilerParams(
            collective_id=0, has_side_effects=True, vmem_limit_bytes=56 * 2**20
        ),
    )(embed_low, embed_high, partner.reshape(1, ROWS), log_scale.reshape(1, 1), bias.reshape(1, 1))
    return grads[:ROWS], grads[ROWS:]


def solution(mesh):
    in_specs = (
        P(("blk", "narrow"), None),
        P(("blk", "narrow"), None),
        P(("blk", "narrow")),
        P(),
        P(),
    )
    out_specs = (P(("blk", "narrow"), None), P(("blk", "narrow"), None))
    return jax.shard_map(
        per_device, mesh=mesh, in_specs=in_specs, out_specs=out_specs, check_vma=False
    )
```

```python
import functools

import jax
import jax.numpy as jnp
from jax import lax
from jax.experimental import pallas as pl
from jax.experimental.pallas import tpu as pltpu
from jax.sharding import PartitionSpec as P

MESH = pl.DeviceIdType.MESH
F32, BF16 = jnp.float32, jnp.bfloat16
X, Y, Z = 4, 4, 8
ROWS, WIDTH = 128, 384
HALF = WIDTH // 2

NEAR = [(0, 0), (1, 0), (3, 0), (0, 1), (0, 3), (2, 0), (0, 2), (1, 1)]
FAR = [(3, 3), (1, 3), (3, 1), (2, 1), (1, 2), (2, 3), (3, 2), (2, 2)]
LOW_AT = {slot: i for i, slot in enumerate(NEAR + FAR)}
HIGH_NEAR = [(0, 0), (0, 1), (1, 0), (7, 0), (1, 1), (7, 1), (6, 0), (2, 0), (6, 1), (2, 1)]
HIGH_FAR = [(4, 0), (4, 1), (3, 0), (3, 1), (5, 0), (5, 1)]
HIGH_AT = {slot: i for i, slot in enumerate(HIGH_NEAR + HIGH_FAR)}
TAIL = 16
STEPS = 32767.0


def dot(a, b, over):
    return lax.dot_general(a, b, (over, ((), ())), preferred_element_type=F32)


def encode(ref, value):
    rows = value.shape[0]
    top = jnp.maximum(jnp.max(jnp.abs(value), axis=0, keepdims=True), 1e-30)
    exponent = jnp.ceil(jnp.log2(top))
    ref[0:rows, :] = jnp.round(value * (STEPS * jnp.exp2(-exponent))).astype(jnp.int32).astype(jnp.int16)
    ref[rows : rows + TAIL, :] = jnp.broadcast_to(exponent, (TAIL, value.shape[1])).astype(jnp.int32).astype(jnp.int16)


def decode(ref):
    rows = ref.shape[0] - TAIL
    exponent = ref[rows : rows + TAIL, :].astype(jnp.int32).astype(F32)[0:1]
    return ref[0:rows, :].astype(jnp.int32).astype(F32) * (jnp.exp2(exponent) * (1.0 / STEPS))


def kernel(
    low_in, high_in, partner_in, log_scale, bias_in,
    out,
    low, high, part, prow, weights, gl, gh,
    ship_a, ship_b, got_a, got_b, next_a, next_b, last_a, last_b,
    got_core, ship_three, ship_four, ship_two, ship_one, got_three, got_four, got_two, got_one,
    load_sems, send_sems, recv_sems,
):
    blk, narrow = lax.axis_index("blk"), lax.axis_index("narrow")
    x, z, y, core = blk // 16, (blk // 2) % 8, (narrow // 2) * 2 + blk % 2, narrow % 2

    def device(dx=0, dy=0, dz=0, dc=0):
        px, py, pz, pc = (x + dx) % X, (y + dy) % Y, (z + dz) % Z, (core + dc) % 2
        return ((px * Z + pz) * 2 + py % 2, (py // 2) * 2 + pc)

    copies = []

    def send(src, dst, **to):
        k = len(copies)
        copy = pltpu.make_async_remote_copy(
            src, dst, send_sems.at[k], recv_sems.at[k], device_id=device(**to), device_id_type=MESH
        )
        copy.start()
        copies.append(copy)
        return copy

    def low_rows(slot, first=0, count=ROWS):
        return pl.ds(LOW_AT[slot] * ROWS + first, count)

    def low_cols(slot):
        return pl.ds(LOW_AT[slot] * ROWS, ROWS)

    def high_rows(dz, dc, first=0, count=ROWS):
        return pl.ds(HIGH_AT[dz, dc] * ROWS + first, count)

    def high_cols(dz, dc):
        return pl.ds(HIGH_AT[dz, dc] * ROWS, ROWS)

    a_rows, b_rows = pl.ds(0, HALF), pl.ds(HALF, HALF)
    own_low, own_high = low.at[low_rows((0, 0))], high.at[high_rows(0, 0)]
    loads = [(low_in, own_low), (high_in, own_high), (partner_in, part.at[0, 0])]
    loads = [pltpu.make_async_copy(src, dst, load_sems.at[i]) for i, (src, dst) in enumerate(loads)]

    peers = [dict(dx=e) for e in (1, 2, 3)] + [dict(dy=e) for e in (1, 2, 3)]
    peers += [dict(dz=e) for e in (1, 2, 6, 7)] + [dict(dc=1)]
    barrier = pltpu.get_barrier_semaphore()
    for peer in peers:
        pl.semaphore_signal(barrier, inc=1, device_id=device(**peer), device_id_type=MESH)
    for load in loads:
        load.start()
    for load in loads:
        load.wait()
    scale = jnp.exp(jnp.full((1, 512), log_scale[0, 0], F32))
    gain, shift, half = 0.5 * scale, 0.5 * bias_in[0, 0], 0.5 * scale
    pl.semaphore_wait(barrier, len(peers))

    low_x, low_y, low_a, low_b, part_x, part_y, high_same, high_other = {}, {}, {}, {}, {}, {}, {}, {}
    for e in (1, 3, 2):
        part_x[4 - e] = send(part.at[0, 0], part.at[0, 4 - e], dx=e)
    for e in (1, 3):
        low_x[4 - e] = send(own_low, low.at[low_rows((4 - e, 0))], dx=e)
        low_y[4 - e] = send(own_low, low.at[low_rows((0, 4 - e))], dy=e)
    for e in (2, 6):
        high_same[8 - e] = send(own_high, high.at[high_rows(8 - e, 0)], dz=e)
    low_x[2] = send(own_low, low.at[low_rows((2, 0))], dx=2)
    low_y[2] = send(own_low, low.at[low_rows((0, 2))], dy=2)
    for e in (1, 7):
        high_same[8 - e] = send(own_high, high.at[high_rows(8 - e, 0)], dz=e)
    high_other[0] = send(own_high, high.at[high_rows(0, 1)], dc=1)

    def to_other_core(dz):
        rows = high_rows(dz, 0)
        high_other[dz] = send(high.at[rows], high.at[high_rows(dz, 1)], dc=1)

    def pass_low(d):
        low_x[d].wait_recv()
        for e in (1, 3, 2):
            src = low.at[low_rows((d, 0), 0, 64)]
            low_a[d, 4 - e] = send(src, low.at[low_rows((d, 4 - e), 0, 64)], dy=e)
        low_y[d].wait_recv()
        for e in (1, 3, 2):
            src = low.at[low_rows((0, d), 64, 64)]
            low_b[4 - e, d] = send(src, low.at[low_rows((4 - e, d), 64, 64)], dx=e)

    for e in (1, 3, 2):
        part_x[e].wait_recv()
    for e in (1, 3, 2):
        part_y[4 - e] = send(part.at[0], part.at[4 - e], dy=e)
    pass_low(1)
    pass_low(3)
    high_same[6].wait_recv()
    high_same[5] = send(high.at[high_rows(6, 0)], high.at[high_rows(5, 0)], dz=1)
    four_a = send(high.at[high_rows(6, 0, 0, 64)], high.at[high_rows(4, 0, 0, 64)], dz=2)
    high_same[2].wait_recv()
    high_same[3] = send(high.at[high_rows(2, 0)], high.at[high_rows(3, 0)], dz=7)
    four_b = send(high.at[high_rows(2, 0, 64, 64)], high.at[high_rows(4, 0, 64, 64)], dz=6)
    pass_low(2)
    for dz in (1, 7):
        high_same[dz].wait_recv()
        to_other_core(dz)
    to_other_core(6)
    to_other_core(2)

    started = set()

    def add_to(ref, index, keys, value):
        if keys <= started:
            ref[index] += value
        else:
            ref[index] = value
            started.update(keys)

    def block(low_slots, high_slots):
        first_low, first_high = LOW_AT[low_slots[0]], HIGH_AT[high_slots[0]]
        wide, tall = len(low_slots) * ROWS, len(high_slots) * ROWS
        cols, rows = pl.ds(first_low * ROWS, wide), pl.ds(first_high * ROWS, tall)
        low_block, high_block = low[cols, :], high[rows, :]
        logits = dot(high_block, low_block, ((1,), (1,)))
        wanted = prow[:, cols]
        for i, (dz, dc) in enumerate(high_slots):
            b, n = device(dz=dz, dc=dc)
            local = wanted - (b * 4 + n) * ROWS
            ids = lax.broadcasted_iota(jnp.int32, (ROWS, 512), 0)
            for left in range(0, wide, 512):
                here = (slice(i * ROWS, (i + 1) * ROWS), slice(left, left + 512))
                match = ids == local[:, left : left + 512]
                value = jnp.tanh(logits[here] * gain + shift) * half + jnp.where(match, -half, half)
                weights[here] = value.astype(BF16)
        w = weights[0:tall, 0:wide]
        add_to(gh, (slice(None), rows), {("h", s) for s in high_slots}, dot(low_block, w, ((0,), (1,))))
        add_to(gl, (slice(None), cols), {("l", s) for s in low_slots}, dot(high_block, w, ((0,), (0,))))

    def take_part(slots):
        for dx, dy in slots:
            prow[:, low_cols((dx, dy))] = part[dy, dx]

    a_first, b_first, a_next, b_next = {}, {}, {}, {}

    def low_first(slots):
        for dx, dy in slots:
            if dy:
                encode(ship_a.at[dy, dx], gl[a_rows, low_cols((dx, dy))])
            if dx:
                encode(ship_b.at[dx, dy], gl[b_rows, low_cols((dx, dy))])
        for dx, dy in slots:
            if dy:
                a_first[4 - dy, dx] = send(ship_a.at[dy, dx], got_a.at[4 - dy, dx], dy=dy)
            if dx:
                b_first[4 - dx, dy] = send(ship_b.at[dx, dy], got_b.at[4 - dx, dy], dx=dx)

    from_core = {}

    def core_sum_send(dz):
        from_core[dz] = send(gh.at[:, high_cols(dz, 1)], got_core.at[dz], dc=1)

    def core_sum_take(dz):
        from_core[dz].wait_recv()
        gh[:, high_cols(dz, 0)] += got_core[dz]

    for e in (1, 2, 3):
        part_y[e].wait_recv()
    take_part(NEAR + FAR)
    high_other[0].wait_recv()
    block(NEAR[:4], HIGH_NEAR[:4])
    low_a[1, 1].wait_recv()
    low_b[1, 1].wait_recv()
    block(NEAR[4:], HIGH_NEAR[:4])
    for dz in (1, 7, 6, 2):
        high_other[dz].wait_recv()
    block(NEAR, HIGH_NEAR[4:])
    for slot in FAR[:4]:
        low_a[slot].wait_recv()
        low_b[slot].wait_recv()
    block(FAR[:4], HIGH_NEAR[:4])
    for dz in (3, 5):
        high_same[dz].wait_recv()
        to_other_core(dz)
    four_a.wait_recv()
    four_b.wait_recv()
    to_other_core(4)
    block(FAR[:4], HIGH_NEAR[4:])
    for slot in FAR[4:]:
        low_a[slot].wait_recv()
        low_b[slot].wait_recv()
    block(FAR[4:], HIGH_NEAR[:6])
    for dz in (1, 7, 0):
        core_sum_send(dz)
    high_other[4].wait_recv()
    high_other[3].wait_recv()
    block(NEAR, HIGH_FAR[:4])
    block(FAR, HIGH_FAR[:4])
    core_sum_send(4)
    core_sum_send(3)
    core_sum_take(1)
    core_sum_take(7)
    encode(ship_one.at[0], gh[:, high_cols(1, 0)])
    encode(ship_one.at[1], gh[:, high_cols(7, 0)])
    one_a = send(ship_one.at[0], got_one.at[0], dz=1)
    one_b = send(ship_one.at[1], got_one.at[1], dz=7)
    high_other[5].wait_recv()
    block(FAR[:4], HIGH_FAR[4:])
    low_first(FAR[:4])
    block(NEAR, HIGH_FAR[4:])
    core_sum_take(4)
    core_sum_take(3)
    encode(ship_four.at[0], gh[a_rows, high_cols(4, 0)])
    encode(ship_four.at[1], gh[b_rows, high_cols(4, 0)])
    encode(ship_three.at[0], gh[:, high_cols(3, 0)])
    four_a = send(ship_four.at[0], got_four.at[0], dz=2)
    four_b = send(ship_four.at[1], got_four.at[1], dz=6)
    three_a = send(ship_three.at[0], got_three.at[0], dz=1)
    low_first(NEAR)
    block(FAR[4:], HIGH_FAR[4:])
    core_sum_send(5)
    block(FAR[4:], HIGH_NEAR[6:])
    core_sum_send(6)
    core_sum_send(2)
    low_first(FAR[4:])
    core_sum_take(5)
    encode(ship_three.at[1], gh[:, high_cols(5, 0)])
    three_b = send(ship_three.at[1], got_three.at[1], dz=7)

    core_sum_take(2)
    core_sum_take(6)
    three_a.wait_recv()
    four_a.wait_recv()
    gh[:, high_cols(2, 0)] += decode(got_three.at[0])
    gh[a_rows, high_cols(2, 0)] += decode(got_four.at[0])
    encode(ship_two.at[0], gh[:, high_cols(2, 0)])
    two_a = send(ship_two.at[0], got_two.at[0], dz=2)
    three_b.wait_recv()
    four_b.wait_recv()
    gh[:, high_cols(6, 0)] += decode(got_three.at[1])
    gh[b_rows, high_cols(6, 0)] += decode(got_four.at[1])
    encode(ship_two.at[1], gh[:, high_cols(6, 0)])
    two_b = send(ship_two.at[1], got_two.at[1], dz=6)
    for d in (1, 3, 2):
        for e in (1, 3, 2):
            a_first[e, d].wait_recv()
        total = gl[a_rows, low_cols((d, 0))]
        for e in (1, 2, 3):
            total += decode(got_a.at[e, d])
        encode(next_a.at[d], total)
        a_next[d] = send(next_a.at[d], last_a.at[d], dx=d)
        for e in (1, 3, 2):
            b_first[e, d].wait_recv()
        total = gl[b_rows, low_cols((0, d))]
        for e in (1, 2, 3):
            total += decode(got_b.at[e, d])
        encode(next_b.at[d], total)
        b_next[d] = send(next_b.at[d], last_b.at[d], dy=d)

    core_sum_take(0)
    one_a.wait_recv()
    one_b.wait_recv()
    total = gh[:, high_cols(0, 0)] + decode(got_one.at[0]) + decode(got_one.at[1])
    total_a, total_b = gl[a_rows, low_cols((0, 0))], gl[b_rows, low_cols((0, 0))]
    for e in (1, 3, 2):
        a_first[e, 0].wait_recv()
        b_first[e, 0].wait_recv()
        total_a += decode(got_a.at[e, 0])
        total_b += decode(got_b.at[e, 0])
    two_a.wait_recv()
    two_b.wait_recv()
    out[ROWS:, :] = (total + decode(got_two.at[0]) + decode(got_two.at[1])).T
    for d in (1, 3, 2):
        a_next[d].wait_recv()
        b_next[d].wait_recv()
        total_a += decode(last_a.at[d])
        total_b += decode(last_b.at[d])
    out[:ROWS, :] = jnp.concatenate([total_a, total_b], axis=0).T
    for copy in copies:
        copy.wait_send()


def per_device(embed_low, embed_high, partner, log_scale, bias):
    hbm, vmem, smem = (pl.BlockSpec(memory_space=m) for m in (pl.ANY, pltpu.VMEM, pltpu.SMEM))
    group = 16 * ROWS
    grads = jax.ShapeDtypeStruct((2 * ROWS, WIDTH), F32)
    half_piece, piece = (HALF + TAIL, ROWS), (WIDTH + TAIL, ROWS)

    def short(*shape):
        return pltpu.VMEM(shape, jnp.int16)

    grads = pl.pallas_call(
        kernel,
        out_shape=grads,
        in_specs=[hbm, hbm, hbm, smem, smem],
        out_specs=vmem,
        scratch_shapes=[
            pltpu.VMEM((group, WIDTH), BF16),
            pltpu.VMEM((group, WIDTH), BF16),
            pltpu.VMEM((4, 4, 1, ROWS), jnp.int32),
            pltpu.VMEM((1, group), jnp.int32),
            pltpu.VMEM((8 * ROWS, 8 * ROWS), BF16),
            pltpu.VMEM((WIDTH, group), F32),
            pltpu.VMEM((WIDTH, group), F32),
            short(4, 4, *half_piece),
            short(4, 4, *half_piece),
            short(4, 4, *half_piece),
            short(4, 4, *half_piece),
            short(4, *half_piece),
            short(4, *half_piece),
            short(4, *half_piece),
            short(4, *half_piece),
            pltpu.VMEM((8, WIDTH, ROWS), F32),
            short(2, *piece),
            short(2, *half_piece),
            short(2, *piece),
            short(2, *piece),
            short(2, *piece),
            short(2, *half_piece),
            short(2, *piece),
            short(2, *piece),
            pltpu.SemaphoreType.DMA((3,)),
            pltpu.SemaphoreType.DMA((96,)),
            pltpu.SemaphoreType.DMA((96,)),
        ],
        compiler_params=pltpu.CompilerParams(
            collective_id=0, has_side_effects=True, vmem_limit_bytes=56 * 2**20
        ),
    )(embed_low, embed_high, partner.reshape(1, ROWS), log_scale.reshape(1, 1), bias.reshape(1, 1))
    return grads[:ROWS], grads[ROWS:]


def solution(mesh):
    in_specs = (
        P(("blk", "narrow"), None),
        P(("blk", "narrow"), None),
        P(("blk", "narrow")),
        P(),
        P(),
    )
    out_specs = (P(("blk", "narrow"), None), P(("blk", "narrow"), None))
    return jax.shard_map(
        per_device, mesh=mesh, in_specs=in_specs, out_specs=out_specs, check_vma=False
    )
```
